256 devices in a mesh: dp: 256 (over y, x, z, core).
Axes of the slice: x: 4, y: 4, z: 8, core: 2. Of those that a mesh axis runs over, the one named last changes fastest.
Arguments:
- images: bfloat16 [131072, 1152], P('dp'), may hold values from -6 to 6
- texts: bfloat16 [131072, 1152], P('dp'), may hold values from -6 to 6
- caption_ids: int32 [131072], P('dp'), may hold values from 0 to 131071
- logit_scale: float32 [1], replicated, may hold values from 4 to 8
- logit_bias: float32 [1], replicated, may hold values from -3 to -1
Outputs:
- grad_images: bfloat16 [131072, 1152], P('dp')
- grad_texts: bfloat16 [131072, 1152], P('dp')
The draws below stay inside these ranges and needn't reach their ends.
All inputs are finite; a program needn't handle non-finite values.
Results may differ from the reference program's by a relative error of at most 0.0095.
Values may be sent and summed in bfloat16 or wider, within the bound.
A program may use at most 64 MiB of HBM per device.

```python
import math
import jax
import jax.numpy as jnp
import numpy as np
from jax import lax

D = 1152
TOK_DEV = 512
ROUNDS = 3
TOKENS = 131072
N_DP = 256


def with_ends(values, rng, low, high):
    shape = values.shape
    place = [jax.random.randint(jax.random.fold_in(rng, axis), (), 0, shape[axis]) for axis in range(len(shape))]
    values = values.at[tuple(place)].set(low)
    longest = shape.index(max(shape))
    place[longest] = (place[longest] + 1) % shape[longest]
    return values.at[tuple(place)].set(high)


def steps_of(own_key, dims, pieces, smallest, top_value):
    factor_of = 1.0
    for axis_at, parts in pieces:
        heights = jax.random.uniform(jax.random.fold_in(jax.random.fold_in(own_key, 6), axis_at), (parts,), jnp.float32, smallest / len(pieces), top_value / len(pieces))
        factor_of = factor_of * jnp.repeat(jnp.exp(heights), dims[axis_at] // parts).reshape((-1,) + (1,) * (len(dims) - 1 - axis_at))
    return factor_of


def wide_ids(own_key, dims, amount, skew):
    portions = [min(1 << octave, amount + 1 - (1 << octave)) * (1 << 20) // math.isqrt((1 << octave) ** skew) + 1 for octave in range((amount + 1).bit_length()) if 1 << octave <= amount]
    scale = 1 + sum(portions) // (1 << 30)
    grid = np.cumsum(np.array([max(1, weight // scale) for weight in portions]))
    ticket = jax.random.randint(jax.random.fold_in(own_key, 1), dims, 0, int(grid[len(portions) - 1]))
    start = jnp.left_shift(1, jnp.searchsorted(jnp.asarray(grid, jnp.int32), ticket, side="right").astype(jnp.int32))
    rank = start - 1 + jax.random.randint(jax.random.fold_in(own_key, 4), dims, 0, 1 << 30) % jnp.minimum(start, amount + 1 - start)
    return jax.random.permutation(jax.random.fold_in(own_key, 2), amount)[rank].astype(jnp.int32)


def centred(own_key, extent, scale, reach, pieces=(), kind=jnp.bfloat16):
    array = jax.random.normal(own_key, extent, jnp.float32) * scale
    if len(pieces) > 0:
        array = steps_of(own_key, extent, pieces, -0.22, 0.18) * array
    return jnp.clip(array, min=-reach, max=reach).astype(kind)


def setup_inputs(seed: int = 0) -> dict:
    key_of = jax.random.split(jax.random.key(seed), 6)
    return {
        "images": centred(key_of[0], (TOKENS, D), 1.0, 6.0, ((0, 256),)),
        "texts": centred(key_of[1], (TOKENS, D), 1.0, 6.0, ((0, 256),)),
        "caption_ids": with_ends(wide_ids(key_of[2], (TOKENS,), TOKENS, 1), jax.random.fold_in(key_of[2], 3), 0, TOKENS - 1).astype(jnp.int32),
        "logit_scale": jnp.clip(jax.random.uniform(key_of[3], (1,), jnp.float32, 4.0, 8.0), 4.0, 8.0),
        "logit_bias": jnp.clip(jax.random.uniform(key_of[4], (1,), jnp.float32, -3.0, -1.0), -3.0, -1.0),
    }


def unit_rows(values):
    wide = values.astype(jnp.float32)
    return (wide / jnp.sqrt(lax.optimization_barrier(jnp.sum(wide * wide, axis=1, keepdims=True)) + 1e-06)).astype(jnp.bfloat16)

def coefficients(left, right, left_ids, right_ids, scale, bias):
    dots = lax.dot_general(left, right, (((1,), (1,)), ((), ())), preferred_element_type=jnp.float32)
    logit = scale * dots + bias
    sign = jnp.where(left_ids[:, None] == right_ids[None, :], jnp.float32(1.0), jnp.float32(-1.0))
    return (-sign * scale * jax.nn.sigmoid(-sign * logit)).astype(jnp.bfloat16)

def reference(images, texts, caption_ids, logit_scale, logit_bias):
    scale = logit_scale[0]
    bias = logit_bias[0]
    img_unit = unit_rows(images).reshape(N_DP, TOK_DEV, D)
    txt_unit = unit_rows(texts).reshape(N_DP, TOK_DEV, D)
    id_blocks = caption_ids.reshape(N_DP, TOK_DEV)
    levels = N_DP.bit_length() - 1

    def one_block(block):
        own_img = img_unit[block]
        own_txt = txt_unit[block]
        own_ids = id_blocks[block]
        coef = coefficients(own_img, own_txt, own_ids, own_ids, scale, bias)
        grad_img = jnp.dot(coef, own_txt, preferred_element_type=jnp.float32)
        grad_txt = lax.dot_general(coef, own_img, (((0,), (0,)), ((), ())), preferred_element_type=jnp.float32)
        for step in range(ROUNDS):
            level = (step + 1) * levels // ROUNDS - 1
            other = jnp.bitwise_xor(block, jnp.int32(1 << level)).astype(jnp.int32)
            far_img = img_unit[other]
            far_txt = txt_unit[other]
            far_ids = id_blocks[other]
            coef = coefficients(own_img, far_txt, own_ids, far_ids, scale, bias)
            grad_img = grad_img + jnp.dot(coef, far_txt, preferred_element_type=jnp.float32)
            back = coefficients(far_img, own_txt, far_ids, own_ids, scale, bias)
            grad_txt = grad_txt + lax.dot_general(back, far_img, (((0,), (0,)), ((), ())), preferred_element_type=jnp.float32)
        return (grad_img.astype(jnp.bfloat16), grad_txt.astype(jnp.bfloat16))
    grad_images, grad_texts = lax.map(one_block, jnp.arange(N_DP, dtype=jnp.int32))
    return (grad_images.reshape(TOKENS, D), grad_texts.reshape(TOKENS, D))
```

```python
import functools

import jax
import jax.numpy as jnp
from jax import lax
from jax.experimental import pallas as pl
from jax.experimental.pallas import tpu as pltpu
from jax.sharding import PartitionSpec as P

ROUNDS = 3
PIECE = 64
GROUP = 128
PER = GROUP // PIECE
PLACED = 1
AHEAD = 2
MESH = pl.DeviceIdType.MESH


def opponents(count):
    levels = count.bit_length() - 1
    me = lax.axis_index("dp")
    found = []
    for step in range(ROUNDS):
        apart = 1 << ((step + 1) * levels // ROUNDS - 1)
        found.append(me + apart - 2 * apart * ((me // apart) % 2))
    return found


def unit_rows(values):
    wide = values.astype(jnp.float32)
    total = jnp.sum(wide * wide, axis=1, keepdims=True) + 1e-06
    return (wide * (1.0 / jnp.sqrt(total))).astype(jnp.bfloat16)


def tournament_kernel(
    count,
    img_in,
    txt_in,
    ids_in,
    scale_ref,
    bias_ref,
    grad_img,
    grad_txt,
    img,
    txt,
    ids,
    ids_column,
    far_txt,
    far_ids,
    terms,
    far_terms,
    img_total,
    txt_total,
    txt_loaded,
    loaded,
    txt_sent,
    txt_here,
    ids_sent,
    ids_here,
    terms_sent,
    terms_here,
):
    rows = img.shape[0]
    pieces = rows // PIECE
    groups = rows // GROUP
    peers = opponents(count)

    def piece(at):
        return pl.ds(pl.multiple_of(at * PIECE, PIECE), PIECE)

    def group(at):
        return pl.ds(pl.multiple_of(at * GROUP, GROUP), GROUP)

    barrier = pltpu.get_barrier_semaphore()
    for peer in peers:
        pl.semaphore_signal(barrier, inc=1, device_id=(peer,), device_id_type=MESH)

    def load_txt(at):
        return pltpu.make_async_copy(txt_in.at[piece(at)], txt.at[piece(at)], txt_loaded.at[at])

    load_ids = pltpu.make_async_copy(ids_in, ids, loaded.at[0])
    load_img = pltpu.make_async_copy(img_in, img, loaded.at[1])
    for at in range(pieces):
        load_txt(at).start()
    load_ids.start()
    load_img.start()

    def send_txt(to, at):
        return pltpu.make_async_remote_copy(
            src_ref=txt.at[piece(at)],
            dst_ref=far_txt.at[to, piece(at)],
            send_sem=txt_sent.at[to, at],
            recv_sem=txt_here.at[to, at],
            device_id=(peers[to],),
            device_id_type=MESH,
        )

    def send_ids(to):
        return pltpu.make_async_remote_copy(
            src_ref=ids,
            dst_ref=far_ids.at[to],
            send_sem=ids_sent.at[to],
            recv_sem=ids_here.at[to],
            device_id=(peers[to],),
            device_id_type=MESH,
        )

    def send_terms(to, at):
        return pltpu.make_async_remote_copy(
            src_ref=terms.at[to, piece(at)],
            dst_ref=far_terms.at[to, piece(at)],
            send_sem=terms_sent.at[to, at],
            recv_sem=terms_here.at[to, at],
            device_id=(peers[to],),
            device_id_type=MESH,
        )

    def start_group(send, at):
        for part in range(PER):
            for to in range(ROUNDS):
                send(to, at * PER + part).start()

    def sent_group(send, at):
        for part in range(PER):
            for to in range(ROUNDS):
                send(to, at * PER + part).wait_send()

    def normalise_txt(at):
        load_txt(at).wait()
        txt[piece(at), :] = unit_rows(txt[piece(at), :])

    normalise_txt(0)
    load_ids.wait()
    pl.semaphore_wait(barrier, ROUNDS)
    for to in range(ROUNDS):
        send_txt(to, 0).start()

    @pl.loop(1, AHEAD * PER)
    def _(at):
        normalise_txt(at)
        for to in range(ROUNDS):
            send_txt(to, at).start()

    for to in range(ROUNDS):
        send_ids(to).start()

    @pl.loop(AHEAD * PER, pieces)
    def _(at):
        normalise_txt(at)

    load_img.wait()

    @pl.loop(0, pieces)
    def _(at):
        img[piece(at), :] = unit_rows(img[piece(at), :])

    scale = scale_ref[0]
    bias = bias_ref[0]
    ids_column[...] = jnp.broadcast_to(ids[...], (128, rows)).T

    def coefficients(right, right_ids):
        dots = lax.dot_general(
            img[...], right, (((1,), (1,)), ((), ())), preferred_element_type=jnp.float32
        )
        logit = scale * dots + bias
        flip = jnp.where(ids_column[:, :1] == right_ids, jnp.float32(-1.0), jnp.float32(1.0))
        return (flip * scale * (1.0 / (1.0 + jnp.exp(-flip * logit)))).astype(jnp.bfloat16)

    def column_terms(coef):
        return lax.dot_general(
            coef, img[...], (((0,), (0,)), ((), ())), preferred_element_type=jnp.float32
        )

    img_total[...] = jnp.zeros_like(img_total)

    @pl.loop(0, groups)
    def _(at):
        right = txt[group(at), :]
        coef = coefficients(right, ids[:, group(at)])
        img_total[...] += jnp.dot(coef, right, preferred_element_type=jnp.float32)
        txt_total[group(at), :] = column_terms(coef)

    for to in range(ROUNDS):
        send_ids(to).wait_recv()

    @pl.loop(0, groups)
    def _(at):
        sent_group(send_txt, at)

        @pl.when(at < groups - AHEAD)
        def _():
            start_group(send_txt, at + AHEAD)

        @pl.when(at >= groups - AHEAD)
        def _():
            start_group(send_terms, at + AHEAD - groups)

        for to in range(ROUNDS):
            for part in range(PER):
                send_txt(to, at * PER + part).wait_recv()
            right = far_txt[to, group(at), :]
            coef = coefficients(right, far_ids[to, :, group(at)])
            terms[to, group(at), :] = column_terms(coef).astype(jnp.bfloat16)
            img_total[...] += jnp.dot(coef, right, preferred_element_type=jnp.float32)

    grad_img[...] = img_total[...].astype(jnp.bfloat16)

    @pl.loop(0, groups)
    def _(at):
        @pl.when(at < groups - AHEAD)
        def _():
            sent_group(send_terms, at)
            start_group(send_terms, at + AHEAD)

        for part in range(PER):
            here = piece(at * PER + part)
            total = txt_total[here, :]
            for to in range(ROUNDS):
                send_terms(to, at * PER + part).wait_recv()
                total = total + far_terms[to, here, :].astype(jnp.float32)
            grad_txt[here, :] = total.astype(jnp.bfloat16)

    for to in range(ROUNDS):
        send_ids(to).wait_send()
    for at in range(groups - AHEAD, groups):
        sent_group(send_terms, at)


def place_kernel(left, right, left_out, right_out, sem):
    copies = []
    for side, (held, placed) in enumerate([(left, left_out), (right, right_out)]):
        for at in range(PLACED):
            part = pl.ds(at * (held.shape[0] // PLACED), held.shape[0] // PLACED)
            copies.append(pltpu.make_async_copy(held.at[part], placed.at[part], sem.at[side, at]))
    for copy in copies:
        copy.start()
    for copy in copies:
        copy.wait()


def body(count, images, texts, caption_ids, logit_scale, logit_bias):
    rows, width = images.shape
    pieces = rows // PIECE
    block = pltpu.VMEM((rows, width), jnp.bfloat16)
    three = pltpu.VMEM((ROUNDS, rows, width), jnp.bfloat16)
    wide = pltpu.VMEM((rows, width), jnp.float32)
    sems = pltpu.SemaphoreType.DMA
    out = jax.ShapeDtypeStruct((rows, width), jnp.bfloat16)
    in_hbm = pl.BlockSpec(memory_space=pltpu.HBM)
    in_vmem = pl.BlockSpec(memory_space=pltpu.VMEM)
    held = [
        pltpu.with_memory_space_constraint(value, pltpu.HBM)
        for value in (images, texts, caption_ids.reshape(1, rows))
    ]
    grads = pl.pallas_call(
        functools.partial(tournament_kernel, count),
        out_shape=(out, out),
        in_specs=[in_hbm] * 3 + [pl.BlockSpec(memory_space=pltpu.SMEM)] * 2,
        out_specs=[in_vmem] * 2,
        scratch_shapes=[
            block,
            block,
            pltpu.VMEM((1, rows), jnp.int32),
            pltpu.VMEM((rows, 128), jnp.int32),
            three,
            pltpu.VMEM((ROUNDS, 1, rows), jnp.int32),
            three,
            three,
            wide,
            wide,
            sems((pieces,)),
            sems((2,)),
            sems((ROUNDS, pieces)),
            sems((ROUNDS, pieces)),
            sems((ROUNDS,)),
            sems((ROUNDS,)),
            sems((ROUNDS, pieces)),
            sems((ROUNDS, pieces)),
        ],
        compiler_params=pltpu.CompilerParams(
            collective_id=0, has_side_effects=True, vmem_limit_bytes=48 * 2**20
        ),
        name="tournament",
    )(*held, logit_scale, logit_bias)
    return pl.pallas_call(
        place_kernel,
        out_shape=(out, out),
        in_specs=[in_vmem] * 2,
        out_specs=[in_hbm] * 2,
        scratch_shapes=[sems((2, PLACED))],
        compiler_params=pltpu.CompilerParams(vmem_limit_bytes=8 * 2**20),
        name="place",
    )(*grads)


def solution(mesh):
    return jax.shard_map(
        functools.partial(body, mesh.shape["dp"]),
        mesh=mesh,
        in_specs=(P("dp", None), P("dp", None), P("dp"), P(), P()),
        out_specs=(P("dp", None), P("dp", None)),
        check_vma=False,
    )
```

```python
import functools

import jax
import jax.numpy as jnp
from jax import lax
from jax.experimental import pallas as pl
from jax.experimental.pallas import tpu as pltpu
from jax.sharding import PartitionSpec as P

ROUNDS = 3
PIECE = 128
GROUP = 128
PER = GROUP // PIECE
STRIP = 32
ADDED = 64
PLACED = 1
AHEAD = 2
MESH = pl.DeviceIdType.MESH


def opponents(count):
    levels = count.bit_length() - 1
    me = lax.axis_index("dp")
    found = []
    for step in range(ROUNDS):
        apart = 1 << ((step + 1) * levels // ROUNDS - 1)
        found.append(me + apart - 2 * apart * ((me // apart) % 2))
    return found


def unit_rows(values):
    wide = values.astype(jnp.float32)
    total = jnp.sum(wide * wide, axis=1, keepdims=True) + 1e-06
    return (wide * (1.0 / jnp.sqrt(total))).astype(jnp.bfloat16)


def tournament_kernel(
    count,
    img_in,
    txt_in,
    ids_in,
    scale_ref,
    bias_ref,
    grad_img,
    grad_txt,
    img,
    txt,
    ids,
    ids_column,
    far_txt,
    far_ids,
    terms,
    far_terms,
    img_total,
    txt_total,
    txt_loaded,
    loaded,
    txt_sent,
    txt_here,
    ids_sent,
    ids_here,
    terms_sent,
    terms_here,
):
    rows = img.shape[0]
    pieces = rows // PIECE
    groups = rows // GROUP
    peers = opponents(count)

    def piece(at):
        return pl.ds(pl.multiple_of(at * PIECE, PIECE), PIECE)

    def group(at):
        return pl.ds(pl.multiple_of(at * GROUP, GROUP), GROUP)

    barrier = pltpu.get_barrier_semaphore()
    for peer in peers:
        pl.semaphore_signal(barrier, inc=1, device_id=(peer,), device_id_type=MESH)

    def load_txt(at):
        return pltpu.make_async_copy(txt_in.at[piece(at)], txt.at[piece(at)], txt_loaded.at[at])

    load_ids = pltpu.make_async_copy(ids_in, ids, loaded.at[0])
    load_img = pltpu.make_async_copy(img_in, img, loaded.at[1])
    for at in range(pieces):
        load_txt(at).start()
    load_ids.start()
    load_img.start()

    def send_txt(to, at, source=txt):
        return pltpu.make_async_remote_copy(
            src_ref=source.at[piece(at)],
            dst_ref=far_txt.at[to, piece(at)],
            send_sem=txt_sent.at[to, at],
            recv_sem=txt_here.at[to, at],
            device_id=(peers[to],),
            device_id_type=MESH,
        )

    def send_ids(to):
        return pltpu.make_async_remote_copy(
            src_ref=ids_in,
            dst_ref=far_ids.at[to],
            send_sem=ids_sent.at[to],
            recv_sem=ids_here.at[to],
            device_id=(peers[to],),
            device_id_type=MESH,
        )

    def send_terms(to, at):
        return pltpu.make_async_remote_copy(
            src_ref=terms.at[to, piece(at)],
            dst_ref=far_terms.at[to, piece(at)],
            send_sem=terms_sent.at[to, at],
            recv_sem=terms_here.at[to, at],
            device_id=(peers[to],),
            device_id_type=MESH,
        )

    def start_group(send, at):
        for part in range(PER):
            for to in range(ROUNDS):
                send(to, at * PER + part).start()

    def sent_group(send, at):
        for part in range(PER):
            for to in range(ROUNDS):
                send(to, at * PER + part).wait_send()

    def normalise(block, start, count):
        @pl.loop(0, count // STRIP)
        def _(at):
            strip = pl.ds(pl.multiple_of(start + at * STRIP, STRIP), STRIP)
            block[strip, :] = unit_rows(block[strip, :])

    pl.semaphore_wait(barrier, ROUNDS)
    for at in range(PER):
        for to in range(ROUNDS):
            send_txt(to, at, txt_in).start()
    for to in range(ROUNDS):
        send_ids(to).start()

    @pl.loop(0, pieces)
    def _(at):
        load_txt(at).wait()
        normalise(txt, at * PIECE, PIECE)

        @pl.when((at >= PER) & (at < AHEAD * PER))
        def _():
            for to in range(ROUNDS):
                send_txt(to, at).start()

    load_img.wait()
    normalise(img, 0, rows)
    load_ids.wait()
    scale = scale_ref[0]
    bias = bias_ref[0]
    ids_column[...] = jnp.broadcast_to(ids[...], (128, rows)).T

    def coefficients(right, right_ids):
        dots = lax.dot_general(
            img[...], right, (((1,), (1,)), ((), ())), preferred_element_type=jnp.float32
        )
        logit = scale * dots + bias
        flip = jnp.where(ids_column[:, :1] == right_ids, jnp.float32(-1.0), jnp.float32(1.0))
        return (flip * scale * (1.0 / (1.0 + jnp.exp(-flip * logit)))).astype(jnp.bfloat16)

    def column_terms(coef):
        return lax.dot_general(
            coef, img[...], (((0,), (0,)), ((), ())), preferred_element_type=jnp.float32
        )

    img_total[...] = jnp.zeros_like(img_total)

    @pl.loop(0, groups)
    def _(at):
        right = txt[group(at), :]
        coef = coefficients(right, ids[:, group(at)])
        img_total[...] += jnp.dot(coef, right, preferred_element_type=jnp.float32)
        txt_total[group(at), :] = column_terms(coef)

    for to in range(ROUNDS):
        send_ids(to).wait_recv()

    @pl.loop(0, groups)
    def _(at):
        sent_group(send_txt, at)

        @pl.when(at < groups - AHEAD)
        def _():
            start_group(send_txt, at + AHEAD)

        @pl.when(at >= groups - AHEAD)
        def _():
            start_group(send_terms, at + AHEAD - groups)

        for to in range(ROUNDS):
            for part in range(PER):
                send_txt(to, at * PER + part).wait_recv()

            @pl.when(at == 0)
            def _():
                normalise(far_txt.at[to], 0, GROUP)

            right = far_txt[to, group(at), :]
            coef = coefficients(right, far_ids[to, :, group(at)])
            terms[to, group(at), :] = column_terms(coef).astype(jnp.bfloat16)
            img_total[...] += jnp.dot(coef, right, preferred_element_type=jnp.float32)

    grad_img[...] = img_total[...].astype(jnp.bfloat16)

    @pl.loop(0, groups)
    def _(at):
        @pl.when(at < groups - AHEAD)
        def _():
            sent_group(send_terms, at)
            start_group(send_terms, at + AHEAD)

        for part in range(PER):
            for to in range(ROUNDS):
                send_terms(to, at * PER + part).wait_recv()

            @pl.loop(0, PIECE // ADDED)
            def _(strip):
                here = pl.ds(
                    pl.multiple_of((at * PER + part) * PIECE + strip * ADDED, ADDED), ADDED
                )
                total = txt_total[here, :]
                for to in range(ROUNDS):
                    total = total + far_terms[to, here, :].astype(jnp.float32)
                grad_txt[here, :] = total.astype(jnp.bfloat16)

    for to in range(ROUNDS):
        send_ids(to).wait_send()
    for at in range(groups - AHEAD, groups):
        sent_group(send_terms, at)


def place_kernel(left, right, left_out, right_out, sem):
    copies = []
    for side, (held, placed) in enumerate([(left, left_out), (right, right_out)]):
        for at in range(PLACED):
            part = pl.ds(at * (held.shape[0] // PLACED), held.shape[0] // PLACED)
            copies.append(pltpu.make_async_copy(held.at[part], placed.at[part], sem.at[side, at]))
    for copy in copies:
        copy.start()
    for copy in copies:
        copy.wait()


def body(count, images, texts, caption_ids, logit_scale, logit_bias):
    rows, width = images.shape
    pieces = rows // PIECE
    block = pltpu.VMEM((rows, width), jnp.bfloat16)
    three = pltpu.VMEM((ROUNDS, rows, width), jnp.bfloat16)
    wide = pltpu.VMEM((rows, width), jnp.float32)
    sems = pltpu.SemaphoreType.DMA
    out = jax.ShapeDtypeStruct((rows, width), jnp.bfloat16)
    in_hbm = pl.BlockSpec(memory_space=pltpu.HBM)
    in_vmem = pl.BlockSpec(memory_space=pltpu.VMEM)
    held = [
        pltpu.with_memory_space_constraint(value, pltpu.HBM)
        for value in (images, texts, caption_ids.reshape(1, rows))
    ]
    grads = pl.pallas_call(
        functools.partial(tournament_kernel, count),
        out_shape=(out, out),
        in_specs=[in_hbm] * 3 + [pl.BlockSpec(memory_space=pltpu.SMEM)] * 2,
        out_specs=[in_vmem] * 2,
        scratch_shapes=[
            block,
            block,
            pltpu.VMEM((1, rows), jnp.int32),
            pltpu.VMEM((rows, 128), jnp.int32),
            three,
            pltpu.VMEM((ROUNDS, 1, rows), jnp.int32),
            three,
            three,
            wide,
            wide,
            sems((pieces,)),
            sems((2,)),
            sems((ROUNDS, pieces)),
            sems((ROUNDS, pieces)),
            sems((ROUNDS,)),
            sems((ROUNDS,)),
            sems((ROUNDS, pieces)),
            sems((ROUNDS, pieces)),
        ],
        compiler_params=pltpu.CompilerParams(
            collective_id=0, has_side_effects=True, vmem_limit_bytes=48 * 2**20
        ),
        name="tournament",
    )(*held, logit_scale, logit_bias)
    return pl.pallas_call(
        place_kernel,
        out_shape=(out, out),
        in_specs=[in_vmem] * 2,
        out_specs=[in_hbm] * 2,
        scratch_shapes=[sems((2, PLACED))],
        compiler_params=pltpu.CompilerParams(vmem_limit_bytes=8 * 2**20),
        name="place",
    )(*grads)


def solution(mesh):
    return jax.shard_map(
        functools.partial(body, mesh.shape["dp"]),
        mesh=mesh,
        in_specs=(P("dp", None), P("dp", None), P("dp"), P(), P()),
        out_specs=(P("dp", None), P("dp", None)),
        check_vma=False,
    )
```

```python
import functools

import jax
import jax.numpy as jnp
from jax import lax
from jax.experimental import pallas as pl
from jax.experimental.pallas import tpu as pltpu
from jax.sharding import PartitionSpec as P

ROUNDS = 3
PIECE = 128
GROUP = 128
PER = GROUP // PIECE
STRIP = 32
ADDED = 64
AHEAD = 2
MESH = pl.DeviceIdType.MESH


def opponents(count):
    levels = count.bit_length() - 1
    me = lax.axis_index("dp")
    found = []
    for step in range(ROUNDS):
        apart = 1 << ((step + 1) * levels // ROUNDS - 1)
        found.append(me + apart - 2 * apart * ((me // apart) % 2))
    return found


def unit_rows(values):
    wide = values.astype(jnp.float32)
    total = jnp.sum(wide * wide, axis=1, keepdims=True) + 1e-06
    return (wide * (1.0 / jnp.sqrt(total))).astype(jnp.bfloat16)


def add_terms(total_ref, terms_ref, result, start, count):
    @pl.loop(0, count // ADDED)
    def _(at):
        here = pl.ds(pl.multiple_of(start + at * ADDED, ADDED), ADDED)
        total = total_ref[here, :]
        for to in range(ROUNDS):
            total = total + terms_ref[to, here, :].astype(jnp.float32)
        result[here, :] = total.astype(jnp.bfloat16)


def tournament_kernel(
    count,
    img_in,
    txt_in,
    ids_in,
    scale_ref,
    bias_ref,
    grad_img,
    grad_txt,
    txt_total,
    far_terms,
    img,
    txt,
    first,
    ids,
    ids_column,
    far_txt,
    far_ids,
    terms,
    img_total,
    txt_loaded,
    loaded,
    txt_sent,
    txt_here,
    ids_sent,
    ids_here,
    terms_sent,
    terms_here,
):
    rows = img.shape[0]
    pieces = rows // PIECE
    groups = rows // GROUP
    peers = opponents(count)

    def piece(at):
        return pl.ds(pl.multiple_of(at * PIECE, PIECE), PIECE)

    def group(at):
        return pl.ds(pl.multiple_of(at * GROUP, GROUP), GROUP)

    barrier = pltpu.get_barrier_semaphore()
    for peer in peers:
        pl.semaphore_signal(barrier, inc=1, device_id=(peer,), device_id_type=MESH)

    def load_txt(at, target=txt):
        return pltpu.make_async_copy(txt_in.at[piece(at)], target.at[piece(at)], txt_loaded.at[at])

    load_ids = pltpu.make_async_copy(ids_in, ids, loaded.at[0])
    load_img = pltpu.make_async_copy(img_in, img, loaded.at[1])
    for at in range(PER):
        load_txt(at, first).start()
    for at in range(PER, pieces):
        load_txt(at).start()
    load_ids.start()
    load_img.start()

    def send_txt(to, at, source=txt):
        return pltpu.make_async_remote_copy(
            src_ref=source.at[piece(at)],
            dst_ref=far_txt.at[to, piece(at)],
            send_sem=txt_sent.at[to, at],
            recv_sem=txt_here.at[to, at],
            device_id=(peers[to],),
            device_id_type=MESH,
        )

    def send_ids(to):
        return pltpu.make_async_remote_copy(
            src_ref=ids_in,
            dst_ref=far_ids.at[to],
            send_sem=ids_sent.at[to],
            recv_sem=ids_here.at[to],
            device_id=(peers[to],),
            device_id_type=MESH,
        )

    def send_terms(to, at):
        return pltpu.make_async_remote_copy(
            src_ref=terms.at[to, piece(at)],
            dst_ref=far_terms.at[to, piece(at)],
            send_sem=terms_sent.at[to, at],
            recv_sem=terms_here.at[to, at],
            device_id=(peers[to],),
            device_id_type=MESH,
        )

    def start_group(send, at):
        for part in range(PER):
            for to in reversed(range(ROUNDS)):
                send(to, at * PER + part).start()

    def sent_group(send, at):
        for part in range(PER):
            for to in range(ROUNDS):
                send(to, at * PER + part).wait_send()

    def normalise(source, block, start, count):
        @pl.loop(0, count // STRIP)
        def _(at):
            strip = pl.ds(pl.multiple_of(start + at * STRIP, STRIP), STRIP)
            block[strip, :] = unit_rows(source[strip, :])

    for at in range(PER):
        load_txt(at, first).wait()
    pl.semaphore_wait(barrier, ROUNDS)
    for at in range(PER):
        for to in reversed(range(ROUNDS)):
            send_txt(to, at, first).start()
    for to in range(ROUNDS):
        send_ids(to).start()

    @pl.loop(PER, pieces)
    def _(at):
        load_txt(at).wait()
        normalise(txt, txt, at * PIECE, PIECE)

        @pl.when(at < AHEAD * PER)
        def _():
            for to in reversed(range(ROUNDS)):
                send_txt(to, at).start()

    normalise(first, txt, 0, GROUP)
    load_img.wait()
    normalise(img, img, 0, rows)
    load_ids.wait()
    scale = scale_ref[0]
    bias = bias_ref[0]
    ids_column[...] = jnp.broadcast_to(ids[...], (128, rows)).T

    def coefficients(right, right_ids):
        dots = lax.dot_general(
            img[...], right, (((1,), (1,)), ((), ())), preferred_element_type=jnp.float32
        )
        logit = scale * dots + bias
        flip = jnp.where(ids_column[:, :1] == right_ids, jnp.float32(-1.0), jnp.float32(1.0))
        return (flip * scale * (1.0 / (1.0 + jnp.exp(-flip * logit)))).astype(jnp.bfloat16)

    def column_terms(coef):
        return lax.dot_general(
            coef, img[...], (((0,), (0,)), ((), ())), preferred_element_type=jnp.float32
        )

    img_total[...] = jnp.zeros_like(img_total)

    @pl.loop(0, groups)
    def _(at):
        right = txt[group(at), :]
        coef = coefficients(right, ids[:, group(at)])
        img_total[...] += jnp.dot(coef, right, preferred_element_type=jnp.float32)
        txt_total[group(at), :] = column_terms(coef)

    for to in range(ROUNDS):
        send_ids(to).wait_recv()

    @pl.loop(0, groups)
    def _(at):
        sent_group(send_txt, at)

        @pl.when(at < groups - AHEAD)
        def _():
            start_group(send_txt, at + AHEAD)

        @pl.when(at >= groups - AHEAD)
        def _():
            start_group(send_terms, at + AHEAD - groups)

        for to in range(ROUNDS):
            for part in range(PER):
                send_txt(to, at * PER + part).wait_recv()

            @pl.when(at == 0)
            def _():
                normalise(far_txt.at[to], far_txt.at[to], 0, GROUP)

            right = far_txt[to, group(at), :]
            coef = coefficients(right, far_ids[to, :, group(at)])
            terms[to, group(at), :] = column_terms(coef).astype(jnp.bfloat16)
            img_total[...] += jnp.dot(coef, right, preferred_element_type=jnp.float32)

    grad_img[...] = img_total[...].astype(jnp.bfloat16)

    @pl.loop(0, groups)
    def _(at):
        @pl.when(at < groups - AHEAD)
        def _():
            sent_group(send_terms, at)
            start_group(send_terms, at + AHEAD)

        for part in range(PER):
            for to in range(ROUNDS):
                send_terms(to, at * PER + part).wait_recv()

            @pl.when(at < groups - 1)
            def _():
                add_terms(txt_total, far_terms, grad_txt, (at * PER + part) * PIECE, PIECE)

    for to in range(ROUNDS):
        send_ids(to).wait_send()
    for at in range(groups - AHEAD, groups):
        sent_group(send_terms, at)


def place_kernel(left, right, total_ref, terms_ref, left_out, right_out, last, sem):
    rows = right.shape[0]
    done = rows - GROUP
    copies = [
        pltpu.make_async_copy(left, left_out, sem.at[0]),
        pltpu.make_async_copy(
            right.at[pl.ds(0, done)], right_out.at[pl.ds(0, done)], sem.at[1]
        ),
    ]
    for copy in copies:
        copy.start()
    for strip in range(GROUP // ADDED):
        here = pl.ds(done + strip * ADDED, ADDED)
        total = total_ref[here, :]
        for to in range(ROUNDS):
            total = total + terms_ref[to, here, :].astype(jnp.float32)
        last[pl.ds(strip * ADDED, ADDED), :] = total.astype(jnp.bfloat16)
    copies.append(pltpu.make_async_copy(last, right_out.at[pl.ds(done, GROUP)], sem.at[2]))
    copies[2].start()
    for copy in copies:
        copy.wait()


def body(count, images, texts, caption_ids, logit_scale, logit_bias):
    rows, width = images.shape
    pieces = rows // PIECE
    block = pltpu.VMEM((rows, width), jnp.bfloat16)
    three = pltpu.VMEM((ROUNDS, rows, width), jnp.bfloat16)
    wide = pltpu.VMEM((rows, width), jnp.float32)
    sems = pltpu.SemaphoreType.DMA
    out = jax.ShapeDtypeStruct((rows, width), jnp.bfloat16)
    in_hbm = pl.BlockSpec(memory_space=pltpu.HBM)
    in_vmem = pl.BlockSpec(memory_space=pltpu.VMEM)
    held = [
        pltpu.with_memory_space_constraint(value, pltpu.HBM)
        for value in (images, texts, caption_ids.reshape(1, rows))
    ]
    grads = pl.pallas_call(
        functools.partial(tournament_kernel, count),
        out_shape=(
            out,
            out,
            jax.ShapeDtypeStruct((rows, width), jnp.float32),
            jax.ShapeDtypeStruct((ROUNDS, rows, width), jnp.bfloat16),
        ),
        in_specs=[in_hbm] * 3 + [pl.BlockSpec(memory_space=pltpu.SMEM)] * 2,
        out_specs=[in_vmem] * 4,
        scratch_shapes=[
            block,
            block,
            pltpu.VMEM((GROUP, width), jnp.bfloat16),
            pltpu.VMEM((1, rows), jnp.int32),
            pltpu.VMEM((rows, 128), jnp.int32),
            three,
            pltpu.VMEM((ROUNDS, 1, rows), jnp.int32),
            three,
            wide,
            sems((pieces,)),
            sems((2,)),
            sems((ROUNDS, pieces)),
            sems((ROUNDS, pieces)),
            sems((ROUNDS,)),
            sems((ROUNDS,)),
            sems((ROUNDS, pieces)),
            sems((ROUNDS, pieces)),
        ],
        compiler_params=pltpu.CompilerParams(
            collective_id=0, has_side_effects=True, vmem_limit_bytes=40 * 2**20
        ),
        name="tournament",
    )(*held, logit_scale, logit_bias)
    return pl.pallas_call(
        place_kernel,
        out_shape=(out, out),
        in_specs=[in_vmem] * 4,
        out_specs=[in_hbm] * 2,
        scratch_shapes=[pltpu.VMEM((GROUP, width), jnp.bfloat16), sems((3,))],
        compiler_params=pltpu.CompilerParams(vmem_limit_bytes=8 * 2**20),
        name="place",
    )(*grads)


def solution(mesh):
    return jax.shard_map(
        functools.partial(body, mesh.shape["dp"]),
        mesh=mesh,
        in_specs=(P("dp", None), P("dp", None), P("dp"), P(), P()),
        out_specs=(P("dp", None), P("dp", None)),
        check_vma=False,
    )
```

```python
import functools

import jax
import jax.numpy as jnp
from jax import lax
from jax.experimental import pallas as pl
from jax.experimental.pallas import tpu as pltpu
from jax.sharding import PartitionSpec as P

ROUNDS = 3
PIECE = 128
GROUP = 128
PER = GROUP // PIECE
STRIP = 32
ADDED = 64
AHEAD = 2
MESH = pl.DeviceIdType.MESH


def opponents(count):
    levels = count.bit_length() - 1
    me = lax.axis_index("dp")
    found = []
    for step in range(ROUNDS):
        apart = 1 << ((step + 1) * levels // ROUNDS - 1)
        found.append(me + apart - 2 * apart * ((me // apart) % 2))
    return found


def unit_rows(values):
    wide = values.astype(jnp.float32)
    total = jnp.sum(wide * wide, axis=1, keepdims=True) + 1e-06
    return (wide * (1.0 / jnp.sqrt(total))).astype(jnp.bfloat16)


def add_terms(total_ref, terms_ref, result, start, count):
    @pl.loop(0, count // ADDED)
    def _(at):
        here = pl.ds(pl.multiple_of(start + at * ADDED, ADDED), ADDED)
        total = total_ref[here, :]
        for to in range(ROUNDS):
            total = total + terms_ref[to, here, :].astype(jnp.float32)
        result[here, :] = total.astype(jnp.bfloat16)


def tournament_kernel(
    count,
    img_in,
    txt_in,
    ids_in,
    scale_ref,
    bias_ref,
    grad_img,
    grad_txt,
    txt_total,
    far_terms,
    img,
    txt,
    first,
    ids,
    ids_column,
    far_txt,
    far_ids,
    terms,
    img_total,
    txt_loaded,
    loaded,
    txt_sent,
    txt_here,
    ids_sent,
    ids_here,
    terms_sent,
    terms_here,
):
    rows = img.shape[0]
    pieces = rows // PIECE
    groups = rows // GROUP
    peers = opponents(count)

    def piece(at):
        return pl.ds(pl.multiple_of(at * PIECE, PIECE), PIECE)

    def group(at):
        return pl.ds(pl.multiple_of(at * GROUP, GROUP), GROUP)

    barrier = pltpu.get_barrier_semaphore()
    for peer in peers:
        pl.semaphore_signal(barrier, inc=1, device_id=(peer,), device_id_type=MESH)

    def load_txt(at, target=txt):
        return pltpu.make_async_copy(txt_in.at[piece(at)], target.at[piece(at)], txt_loaded.at[at])

    load_ids = pltpu.make_async_copy(ids_in, ids, loaded.at[0])
    load_img = pltpu.make_async_copy(img_in, img, loaded.at[1])
    for at in range(PER):
        load_txt(at, first).start()
    for at in range(PER, pieces):
        load_txt(at).start()
    load_ids.start()
    load_img.start()

    def send_txt(to, at, source=txt):
        return pltpu.make_async_remote_copy(
            src_ref=source.at[piece(at)],
            dst_ref=far_txt.at[to, piece(at)],
            send_sem=txt_sent.at[to, at],
            recv_sem=txt_here.at[to, at],
            device_id=(peers[to],),
            device_id_type=MESH,
        )

    def send_ids(to):
        return pltpu.make_async_remote_copy(
            src_ref=ids_in,
            dst_ref=far_ids.at[to],
            send_sem=ids_sent.at[to],
            recv_sem=ids_here.at[to],
            device_id=(peers[to],),
            device_id_type=MESH,
        )

    def send_terms(to, at):
        return pltpu.make_async_remote_copy(
            src_ref=terms.at[to, piece(at)],
            dst_ref=far_terms.at[to, piece(at)],
            send_sem=terms_sent.at[to, at],
            recv_sem=terms_here.at[to, at],
            device_id=(peers[to],),
            device_id_type=MESH,
        )

    def next_group(left, left_at, send, at):
        for to in range(ROUNDS):
            for part in range(PER):
                left(to, left_at * PER + part).wait_send()
            for part in range(PER):
                send(to, at * PER + part).start()

    def sent_group(send, at):
        for part in range(PER):
            for to in range(ROUNDS):
                send(to, at * PER + part).wait_send()

    def normalise(source, block, start, count):
        @pl.loop(0, count // STRIP)
        def _(at):
            strip = pl.ds(pl.multiple_of(start + at * STRIP, STRIP), STRIP)
            block[strip, :] = unit_rows(source[strip, :])

    for at in range(PER):
        load_txt(at, first).wait()
    pl.semaphore_wait(barrier, ROUNDS)
    for at in range(PER):
        for to in reversed(range(ROUNDS)):
            send_txt(to, at, first).start()
    for to in range(ROUNDS):
        send_ids(to).start()

    @pl.loop(PER, pieces)
    def _(at):
        load_txt(at).wait()
        normalise(txt, txt, at * PIECE, PIECE)

        @pl.when(at < AHEAD * PER)
        def _():
            for to in reversed(range(ROUNDS)):
                send_txt(to, at).start()

    normalise(first, txt, 0, GROUP)
    load_img.wait()
    normalise(img, img, 0, rows)
    load_ids.wait()
    scale = scale_ref[0]
    bias = bias_ref[0]
    ids_column[...] = jnp.broadcast_to(ids[...], (128, rows)).T

    def coefficients(right, right_ids):
        dots = lax.dot_general(
            img[...], right, (((1,), (1,)), ((), ())), preferred_element_type=jnp.float32
        )
        logit = scale * dots + bias
        flip = jnp.where(ids_column[:, :1] == right_ids, jnp.float32(-1.0), jnp.float32(1.0))
        return (flip * scale * (1.0 / (1.0 + jnp.exp(-flip * logit)))).astype(jnp.bfloat16)

    def column_terms(coef):
        return lax.dot_general(
            coef, img[...], (((0,), (0,)), ((), ())), preferred_element_type=jnp.float32
        )

    img_total[...] = jnp.zeros_like(img_total)

    @pl.loop(0, groups)
    def _(at):
        right = txt[group(at), :]
        coef = coefficients(right, ids[:, group(at)])
        img_total[...] += jnp.dot(coef, right, preferred_element_type=jnp.float32)
        txt_total[group(at), :] = column_terms(coef)

    for to in range(ROUNDS):
        send_ids(to).wait_recv()

    @pl.loop(0, groups)
    def _(at):
        @pl.when(at < groups - AHEAD)
        def _():
            next_group(send_txt, at, send_txt, at + AHEAD)

        @pl.when(at >= groups - AHEAD)
        def _():
            next_group(send_txt, at, send_terms, at + AHEAD - groups)

        for to in range(ROUNDS):
            for part in range(PER):
                send_txt(to, at * PER + part).wait_recv()

            @pl.when(at == 0)
            def _():
                normalise(far_txt.at[to], far_txt.at[to], 0, GROUP)

            right = far_txt[to, group(at), :]
            coef = coefficients(right, far_ids[to, :, group(at)])
            terms[to, group(at), :] = column_terms(coef).astype(jnp.bfloat16)
            img_total[...] += jnp.dot(coef, right, preferred_element_type=jnp.float32)

    grad_img[...] = img_total[...].astype(jnp.bfloat16)

    @pl.loop(0, groups)
    def _(at):
        @pl.when(at < groups - AHEAD)
        def _():
            next_group(send_terms, at, send_terms, at + AHEAD)

        for part in range(PER):
            for to in range(ROUNDS):
                send_terms(to, at * PER + part).wait_recv()

            @pl.when(at < groups - 1)
            def _():
                add_terms(txt_total, far_terms, grad_txt, (at * PER + part) * PIECE, PIECE)

    for to in range(ROUNDS):
        send_ids(to).wait_send()
    for at in range(groups - AHEAD, groups):
        sent_group(send_terms, at)


def place_kernel(left, right, total_ref, terms_ref, left_out, right_out, last, sem):
    rows = right.shape[0]
    done = rows - GROUP
    copies = [
        pltpu.make_async_copy(left, left_out, sem.at[0]),
        pltpu.make_async_copy(
            right.at[pl.ds(0, done)], right_out.at[pl.ds(0, done)], sem.at[1]
        ),
    ]
    for copy in copies:
        copy.start()
    for strip in range(GROUP // ADDED):
        here = pl.ds(done + strip * ADDED, ADDED)
        total = total_ref[here, :]
        for to in range(ROUNDS):
            total = total + terms_ref[to, here, :].astype(jnp.float32)
        last[pl.ds(strip * ADDED, ADDED), :] = total.astype(jnp.bfloat16)
    copies.append(pltpu.make_async_copy(last, right_out.at[pl.ds(done, GROUP)], sem.at[2]))
    copies[2].start()
    for copy in copies:
        copy.wait()


def body(count, images, texts, caption_ids, logit_scale, logit_bias):
    rows, width = images.shape
    pieces = rows // PIECE
    block = pltpu.VMEM((rows, width), jnp.bfloat16)
    three = pltpu.VMEM((ROUNDS, rows, width), jnp.bfloat16)
    wide = pltpu.VMEM((rows, width), jnp.float32)
    sems = pltpu.SemaphoreType.DMA
    out = jax.ShapeDtypeStruct((rows, width), jnp.bfloat16)
    in_hbm = pl.BlockSpec(memory_space=pltpu.HBM)
    in_vmem = pl.BlockSpec(memory_space=pltpu.VMEM)
    held = [
        pltpu.with_memory_space_constraint(value, pltpu.HBM)
        for value in (images, texts, caption_ids.reshape(1, rows))
    ]
    grads = pl.pallas_call(
        functools.partial(tournament_kernel, count),
        out_shape=(
            out,
            out,
            jax.ShapeDtypeStruct((rows, width), jnp.float32),
            jax.ShapeDtypeStruct((ROUNDS, rows, width), jnp.bfloat16),
        ),
        in_specs=[in_hbm] * 3 + [pl.BlockSpec(memory_space=pltpu.SMEM)] * 2,
        out_specs=[in_vmem] * 4,
        scratch_shapes=[
            block,
            block,
            pltpu.VMEM((GROUP, width), jnp.bfloat16),
            pltpu.VMEM((1, rows), jnp.int32),
            pltpu.VMEM((rows, 128), jnp.int32),
            three,
            pltpu.VMEM((ROUNDS, 1, rows), jnp.int32),
            three,
            wide,
            sems((pieces,)),
            sems((2,)),
            sems((ROUNDS, pieces)),
            sems((ROUNDS, pieces)),
            sems((ROUNDS,)),
            sems((ROUNDS,)),
            sems((ROUNDS, pieces)),
            sems((ROUNDS, pieces)),
        ],
        compiler_params=pltpu.CompilerParams(
            collective_id=0, has_side_effects=True, vmem_limit_bytes=40 * 2**20
        ),
        name="tournament",
    )(*held, logit_scale, logit_bias)
    return pl.pallas_call(
        place_kernel,
        out_shape=(out, out),
        in_specs=[in_vmem] * 4,
        out_specs=[in_hbm] * 2,
        scratch_shapes=[pltpu.VMEM((GROUP, width), jnp.bfloat16), sems((3,))],
        compiler_params=pltpu.CompilerParams(vmem_limit_bytes=8 * 2**20),
        name="place",
    )(*grads)


def solution(mesh):
    return jax.shard_map(
        functools.partial(body, mesh.shape["dp"]),
        mesh=mesh,
        in_specs=(P("dp", None), P("dp", None), P("dp"), P(), P()),
        out_specs=(P("dp", None), P("dp", None)),
        check_vma=False,
    )
```

```python
import functools

import jax
import jax.numpy as jnp
from jax import lax
from jax.experimental import pallas as pl
from jax.experimental.pallas import tpu as pltpu
from jax.sharding import PartitionSpec as P

ROUNDS = 3
PIECE = 128
GROUP = 128
PER = GROUP // PIECE
STRIP = 32
ADDED = 64
AHEAD = 2
MESH = pl.DeviceIdType.MESH


def opponents(count):
    levels = count.bit_length() - 1
    me = lax.axis_index("dp")
    found = []
    for step in range(ROUNDS):
        apart = 1 << ((step + 1) * levels // ROUNDS - 1)
        found.append(me + apart - 2 * apart * ((me // apart) % 2))
    return found


def unit_rows(values):
    wide = values.astype(jnp.float32)
    total = jnp.sum(wide * wide, axis=1, keepdims=True) + 1e-06
    return (wide * (1.0 / jnp.sqrt(total))).astype(jnp.bfloat16)


def add_terms(total_ref, terms_ref, result, start, count):
    @pl.loop(0, count // ADDED)
    def _(at):
        here = pl.ds(pl.multiple_of(start + at * ADDED, ADDED), ADDED)
        total = total_ref[here, :]
        for to in range(ROUNDS):
            total = total + terms_ref[to, here, :].astype(jnp.float32)
        result[here, :] = total.astype(jnp.bfloat16)


def tournament_kernel(
    count,
    img_in,
    txt_in,
    ids_in,
    scale_ref,
    bias_ref,
    grad_img,
    grad_txt,
    txt_total,
    far_terms,
    img,
    txt,
    first,
    ids,
    ids_column,
    far_txt,
    far_ids,
    terms,
    img_total,
    txt_loaded,
    loaded,
    txt_sent,
    txt_here,
    ids_sent,
    ids_here,
    terms_sent,
    terms_here,
):
    rows = img.shape[0]
    pieces = rows // PIECE
    groups = rows // GROUP
    peers = opponents(count)

    def piece(at):
        return pl.ds(pl.multiple_of(at * PIECE, PIECE), PIECE)

    def group(at):
        return pl.ds(pl.multiple_of(at * GROUP, GROUP), GROUP)

    barrier = pltpu.get_barrier_semaphore()
    for peer in peers:
        pl.semaphore_signal(barrier, inc=1, device_id=(peer,), device_id_type=MESH)

    def load_txt(at, target=txt):
        return pltpu.make_async_copy(txt_in.at[piece(at)], target.at[piece(at)], txt_loaded.at[at])

    load_ids = pltpu.make_async_copy(ids_in, ids, loaded.at[0])
    load_img = pltpu.make_async_copy(img_in, img, loaded.at[1])
    for at in range(PER):
        load_txt(at, first).start()
    for at in range(PER, pieces):
        load_txt(at).start()
    load_ids.start()
    load_img.start()

    def send_txt(to, at, source=txt):
        return pltpu.make_async_remote_copy(
            src_ref=source.at[piece(at)],
            dst_ref=far_txt.at[to, piece(at)],
            send_sem=txt_sent.at[to, at],
            recv_sem=txt_here.at[to, at],
            device_id=(peers[to],),
            device_id_type=MESH,
        )

    def send_ids(to):
        return pltpu.make_async_remote_copy(
            src_ref=ids_in,
            dst_ref=far_ids.at[to],
            send_sem=ids_sent.at[to],
            recv_sem=ids_here.at[to],
            device_id=(peers[to],),
            device_id_type=MESH,
        )

    def send_terms(to, at):
        return pltpu.make_async_remote_copy(
            src_ref=terms.at[to, piece(at)],
            dst_ref=far_terms.at[to, piece(at)],
            send_sem=terms_sent.at[to, at],
            recv_sem=terms_here.at[to, at],
            device_id=(peers[to],),
            device_id_type=MESH,
        )

    def start_group(send, at):
        for part in range(PER):
            for to in reversed(range(ROUNDS)):
                send(to, at * PER + part).start()

    def sent_group(send, at):
        for part in range(PER):
            for to in range(ROUNDS):
                send(to, at * PER + part).wait_send()

    def normalise(source, block, start, count):
        @pl.loop(0, count // STRIP)
        def _(at):
            strip = pl.ds(pl.multiple_of(start + at * STRIP, STRIP), STRIP)
            block[strip, :] = unit_rows(source[strip, :])

    for at in range(PER):
        load_txt(at, first).wait()
    pl.semaphore_wait(barrier, ROUNDS)
    for at in range(PER):
        for to in reversed(range(ROUNDS)):
            send_txt(to, at, first).start()
    for to in range(ROUNDS):
        send_ids(to).start()

    @pl.loop(PER, pieces)
    def _(at):
        load_txt(at).wait()
        normalise(txt, txt, at * PIECE, PIECE)

        @pl.when(at < AHEAD * PER)
        def _():
            for to in reversed(range(ROUNDS)):
                send_txt(to, at).start()

    normalise(first, txt, 0, GROUP)
    load_img.wait()
    normalise(img, img, 0, rows)
    load_ids.wait()
    scale = scale_ref[0]
    bias = bias_ref[0]
    ids_column[...] = jnp.broadcast_to(ids[...], (128, rows)).T

    def coefficients(right, right_ids):
        dots = lax.dot_general(
            img[...], right, (((1,), (1,)), ((), ())), preferred_element_type=jnp.float32
        )
        logit = scale * dots + bias
        flip = jnp.where(ids_column[:, :1] == right_ids, jnp.float32(-1.0), jnp.float32(1.0))
        return (flip * scale * (1.0 / (1.0 + jnp.exp(-flip * logit)))).astype(jnp.bfloat16)

    def column_terms(coef):
        return lax.dot_general(
            coef, img[...], (((0,), (0,)), ((), ())), preferred_element_type=jnp.float32
        )

    img_total[...] = jnp.zeros_like(img_total)

    @pl.loop(0, groups)
    def _(at):
        right = txt[group(at), :]
        coef = coefficients(right, ids[:, group(at)])
        img_total[...] += jnp.dot(coef, right, preferred_element_type=jnp.float32)
        txt_total[group(at), :] = column_terms(coef)

    for to in range(ROUNDS):
        send_ids(to).wait_recv()

    @pl.loop(0, groups)
    def _(at):
        sent_group(send_txt, at)

        @pl.when(at < groups - AHEAD)
        def _():
            start_group(send_txt, at + AHEAD)

        @pl.when(at >= groups - AHEAD)
        def _():
            start_group(send_terms, at + AHEAD - groups)

        for to in range(ROUNDS):
            for part in range(PER):
                send_txt(to, at * PER + part).wait_recv()

            @pl.when(at == 0)
            def _():
                normalise(far_txt.at[to], far_txt.at[to], 0, GROUP)

            right = far_txt[to, group(at), :]
            coef = coefficients(right, far_ids[to, :, group(at)])
            terms[to, group(at), :] = column_terms(coef).astype(jnp.bfloat16)
            img_total[...] += jnp.dot(coef, right, preferred_element_type=jnp.float32)


    @pl.loop(0, groups)
    def _(at):
        @pl.when(at == 0)
        def _():
            start_group(send_terms, AHEAD)
            sent_group(send_terms, 0)
            start_group(send_terms, AHEAD + 1)
            sent_group(send_terms, 1)

        grad_img[group(at), :] = img_total[group(at), :].astype(jnp.bfloat16)

        for part in range(PER):
            for to in range(ROUNDS):
                send_terms(to, at * PER + part).wait_recv()

            @pl.when(at < groups - 1)
            def _():
                add_terms(txt_total, far_terms, grad_txt, (at * PER + part) * PIECE, PIECE)

    for to in range(ROUNDS):
        send_ids(to).wait_send()
    for at in range(groups - AHEAD, groups):
        sent_group(send_terms, at)


def place_kernel(left, right, total_ref, terms_ref, left_out, right_out, last, sem):
    rows = right.shape[0]
    done = rows - GROUP
    copies = [
        pltpu.make_async_copy(left, left_out, sem.at[0]),
        pltpu.make_async_copy(
            right.at[pl.ds(0, done)], right_out.at[pl.ds(0, done)], sem.at[1]
        ),
    ]
    for copy in copies:
        copy.start()
    for strip in range(GROUP // ADDED):
        here = pl.ds(done + strip * ADDED, ADDED)
        total = total_ref[here, :]
        for to in range(ROUNDS):
            total = total + terms_ref[to, here, :].astype(jnp.float32)
        last[pl.ds(strip * ADDED, ADDED), :] = total.astype(jnp.bfloat16)
    copies.append(pltpu.make_async_copy(last, right_out.at[pl.ds(done, GROUP)], sem.at[2]))
    copies[2].start()
    for copy in copies:
        copy.wait()


def body(count, images, texts, caption_ids, logit_scale, logit_bias):
    rows, width = images.shape
    pieces = rows // PIECE
    block = pltpu.VMEM((rows, width), jnp.bfloat16)
    three = pltpu.VMEM((ROUNDS, rows, width), jnp.bfloat16)
    wide = pltpu.VMEM((rows, width), jnp.float32)
    sems = pltpu.SemaphoreType.DMA
    out = jax.ShapeDtypeStruct((rows, width), jnp.bfloat16)
    in_hbm = pl.BlockSpec(memory_space=pltpu.HBM)
    in_vmem = pl.BlockSpec(memory_space=pltpu.VMEM)
    held = [
        pltpu.with_memory_space_constraint(value, pltpu.HBM)
        for value in (images, texts, caption_ids.reshape(1, rows))
    ]
    grads = pl.pallas_call(
        functools.partial(tournament_kernel, count),
        out_shape=(
            out,
            out,
            jax.ShapeDtypeStruct((rows, width), jnp.float32),
            jax.ShapeDtypeStruct((ROUNDS, rows, width), jnp.bfloat16),
        ),
        in_specs=[in_hbm] * 3 + [pl.BlockSpec(memory_space=pltpu.SMEM)] * 2,
        out_specs=[in_vmem] * 4,
        scratch_shapes=[
            block,
            block,
            pltpu.VMEM((GROUP, width), jnp.bfloat16),
            pltpu.VMEM((1, rows), jnp.int32),
            pltpu.VMEM((rows, 128), jnp.int32),
            three,
            pltpu.VMEM((ROUNDS, 1, rows), jnp.int32),
            three,
            wide,
            sems((pieces,)),
            sems((2,)),
            sems((ROUNDS, pieces)),
            sems((ROUNDS, pieces)),
            sems((ROUNDS,)),
            sems((ROUNDS,)),
            sems((ROUNDS, pieces)),
            sems((ROUNDS, pieces)),
        ],
        compiler_params=pltpu.CompilerParams(
            collective_id=0, has_side_effects=True, vmem_limit_bytes=40 * 2**20
        ),
        name="tournament",
    )(*held, logit_scale, logit_bias)
    return pl.pallas_call(
        place_kernel,
        out_shape=(out, out),
        in_specs=[in_vmem] * 4,
        out_specs=[in_hbm] * 2,
        scratch_shapes=[pltpu.VMEM((GROUP, width), jnp.bfloat16), sems((3,))],
        compiler_params=pltpu.CompilerParams(vmem_limit_bytes=8 * 2**20),
        name="place",
    )(*grads)


def solution(mesh):
    return jax.shard_map(
        functools.partial(body, mesh.shape["dp"]),
        mesh=mesh,
        in_specs=(P("dp", None), P("dp", None), P("dp"), P(), P()),
        out_specs=(P("dp", None), P("dp", None)),
        check_vma=False,
    )
```
